32 devices in a mesh: blk: 8 (over y, x, core), grp: 4 (over z).
Axes of the slice: x: 2, y: 2, z: 4, core: 2. Of those that a mesh axis runs over, the one named last changes fastest.
Arguments:
- queries: bfloat16 [8, 640, 3072], P('blk', 'grp'), may hold values from -200 to 200
- keys: bfloat16 [8, 640, 3072], P('blk', 'grp'), may hold values from -6 to 6
- values: bfloat16 [8, 640, 3072], P('blk', 'grp'), may hold values from -6 to 6
- head_kind: int32 [24], replicated, may hold values from 0 to 1, as said below
- frame_reach: int32 [24], replicated, may hold values from 1 to 7
Outputs:
- attended: bfloat16 [8, 640, 3072], P('blk', 'grp')
The draws below stay inside these ranges and needn't reach their ends.
Inputs may be any that keep to these rules, and one draw needn't show every extreme that they name: `head_kind`: exactly 16 of the 24 heads are 0, the others are 1.
All inputs are finite; a program needn't handle non-finite values.
Results may differ from the reference program's by a relative error of at most 0.0065.
Values may be sent and summed in bfloat16 or wider, within the bound.
A program may use at most 128 MiB of HBM per device.

```python
import jax
import jax.numpy as jnp
from jax import lax

H = 24
HD = 128
D = 3072
HS = 16
FRAMES = 8
POSITIONS = 640


def shared_keys(key):
    base = jax.random.normal(key, (FRAMES, POSITIONS, H * HD), jnp.float32)
    return jnp.clip(base, -6.0, 6.0)


def draw_queries(key, part):
    common = shared_keys(key)
    key = jax.random.fold_in(key, 11)
    fresh = jnp.clip(jax.random.normal(key, common.shape, jnp.float32), -6.0, 6.0)
    return fresh.astype(jnp.bfloat16)


def draw_keys(key, part):
    common = shared_keys(key)
    return common.astype(jnp.bfloat16)


def draw_head_kind(key, part):
    key = jax.random.fold_in(key, 17)
    shuffled = jax.random.permutation(key, H)
    return (shuffled >= HS).astype(jnp.int32)


def touch_ends(entries, own_key, smallest, high):
    extent = entries.shape
    index_at = [jax.random.randint(jax.random.fold_in(own_key, axis), (), 0, extent[axis]) for axis in range(len(extent))]
    entries = entries.at[tuple(index_at)].set(smallest)
    longest = extent.index(max(extent))
    index_at[longest] = (index_at[longest] + 1) % extent[longest]
    return entries.at[tuple(index_at)].set(high)


def level_of(own_key, extent, split, least, top_value):
    loudness, own = 1.0, jax.random.fold_in(own_key, 6)
    for axis_at, parts in split:
        draws = jnp.exp(jax.random.uniform(jax.random.fold_in(own, axis_at), (parts,), jnp.float32, least / len(split), top_value / len(split)))
        loudness = loudness * jnp.repeat(draws, extent[axis_at] // parts).reshape([-1 if axis == axis_at else 1 for axis in range(len(extent))])
    return loudness


def bell_draw(stream_key, dims, width, limit, cuts=(), kind=jnp.bfloat16):
    entries = jax.random.normal(stream_key, dims, jnp.float32) * width
    if len(cuts) > 0:
        entries = level_of(stream_key, dims, cuts, -0.22, 0.18) * entries
    return jnp.clip(entries, min=-limit, max=limit).astype(kind)


def setup_inputs(seed: int = 0) -> dict:
    splits = jax.random.split(jax.random.key(seed), 6)
    return {
        "queries": draw_queries(jax.random.fold_in(splits[5], 71), 0),
        "keys": draw_keys(jax.random.fold_in(splits[5], 71), 0),
        "values": bell_draw(splits[2], (FRAMES, POSITIONS, D), 1.0, 6.0, ((0, 8), (1, 4))),
        "head_kind": draw_head_kind(jax.random.fold_in(splits[5], 71), 0),
        "frame_reach": touch_ends(jax.random.randint(splits[4], (H,), 1, FRAMES), jax.random.fold_in(splits[4], 1), 1, FRAMES - 1).astype(jnp.int32),
    }


def reference(queries, keys, values, head_kind, frame_reach):
    order = jnp.argsort(head_kind, stable=True).astype(jnp.int32)
    inverse = jnp.argsort(order).astype(jnp.int32)
    factor = HD ** -0.5

    def arrange(tensor):
        return jnp.take(tensor.reshape(FRAMES, POSITIONS, H, HD), order, axis=2)

    query_heads = arrange(queries)
    key_heads = arrange(keys)
    value_heads = arrange(values)

    def one_head(inputs):
        query_one, key_one, value_one = inputs
        scores = jnp.dot(query_one, key_one.T, preferred_element_type=jnp.float32) * factor
        weights = jnp.exp(scores - jnp.max(scores, axis=-1, keepdims=True))
        rounded = weights.astype(jnp.bfloat16)
        summed = jnp.dot(rounded, value_one, preferred_element_type=jnp.float32)
        return summed / jnp.sum(weights, axis=-1, keepdims=True)

    def one_frame(inputs):
        query_frame, key_frame, value_frame = inputs
        return lax.map(one_head, (jnp.transpose(query_frame[:, :HS], (1, 0, 2)),
                                  jnp.transpose(key_frame[:, :HS], (1, 0, 2)),
                                  jnp.transpose(value_frame[:, :HS], (1, 0, 2))))

    spatial = lax.map(one_frame, (query_heads, key_heads, value_heads))
    spatial = jnp.transpose(spatial, (0, 2, 1, 3))

    reach_sorted = jnp.take(frame_reach, order)[HS:]
    frame_ids = jnp.arange(FRAMES, dtype=jnp.int32)
    distance = jnp.abs(frame_ids[:, None] - frame_ids[None, :])
    allowed = (distance[None, :, :] <= reach_sorted[:, None, None])[None]
    query_time = query_heads[:, :, HS:].astype(jnp.float32)
    key_time = key_heads[:, :, HS:].astype(jnp.float32)
    value_time = value_heads[:, :, HS:].astype(jnp.float32)
    scores = jnp.einsum("fphd,gphd->phfg", query_time, key_time) * factor
    scores = jnp.where(allowed, scores, -1e30)
    largest = jnp.max(scores, axis=-1, keepdims=True)
    weights = jnp.where(allowed, jnp.exp(scores - largest), 0.0)
    rounded = lax.optimization_barrier(weights.astype(jnp.bfloat16))
    summed = jnp.einsum("phfg,gphd->phfd", rounded.astype(jnp.float32), value_time)
    temporal = summed / jnp.sum(weights, axis=-1)[..., None]
    temporal = jnp.transpose(temporal, (2, 0, 1, 3))

    joined = jnp.concatenate([spatial, temporal], axis=2)
    joined = jnp.take(joined, inverse, axis=2)
    return joined.reshape(FRAMES, POSITIONS, H * HD).astype(jnp.bfloat16)
```

```python
import functools

import jax
import jax.numpy as jnp
from jax import lax
from jax.experimental import pallas as pl
from jax.experimental.pallas import tpu as pltpu
from jax.sharding import PartitionSpec as P

HS = 16
MESH = pl.DeviceIdType.MESH


def flip(me, other, size):
    total, place = 0, 1
    while place < size:
        mine = lax.rem(lax.div(me, jnp.int32(place)), jnp.int32(2))
        if isinstance(other, int):
            digit = (other // place) % 2
            changed = 1 - mine if digit else mine
        else:
            digit = lax.rem(lax.div(other, jnp.int32(place)), jnp.int32(2))
            changed = lax.rem(mine + digit, jnp.int32(2))
        total = total + place * changed
        place *= 2
    return total


def far_first(size):
    return [(step + size // 2) % size for step in range(size) if (step + size // 2) % size]


def weighted(q, k, v, factor, allowed=None):
    scores = lax.dot_general(q, k, (((1,), (1,)), ((), ())), preferred_element_type=jnp.float32)
    if allowed is not None:
        scores = jnp.where(allowed, scores, -1e30)
    top = jnp.max(scores, axis=-1, keepdims=True)
    weights = jnp.exp((scores - top) * factor)
    total = jnp.sum(weights, axis=-1, keepdims=True)
    summed = jnp.dot(weights.astype(jnp.bfloat16), v, preferred_element_type=jnp.float32)
    return (summed / total).astype(jnp.bfloat16)


def kernel(
    groups, frames,
    q_hbm, k_hbm, v_hbm, kind_ref, reach_ref, out_ref,
    stage, packed, packed_time, seen, seen_time, made, made_time, result, order, inverse,
    load_sem, space_send, space_recv, back_send, back_recv,
    time_send, time_recv, home_send, home_recv,
):
    heads = kind_ref.shape[0]
    places = stage.shape[2]
    size = stage.shape[3]
    owned = HS // groups
    splits = frames // (heads - HS)
    rows = places // splits
    factor = size ** (-0.5)
    me = lax.axis_index("grp")
    frame = lax.axis_index("blk")
    space_peers = far_first(groups)
    time_peers = far_first(frames)

    barrier = pltpu.get_barrier_semaphore()
    for d in space_peers:
        pl.semaphore_signal(
            barrier, inc=1, device_id={"grp": flip(me, d, groups)}, device_id_type=MESH
        )
    for d in time_peers:
        pl.semaphore_signal(
            barrier, inc=1, device_id={"blk": flip(frame, d, frames)}, device_id_type=MESH
        )
    loads = [
        pltpu.make_async_copy(
            source.at[:, h * size : (h + 1) * size], stage.at[part, h], load_sem.at[part, h]
        )
        for h in range(heads)
        for part, source in enumerate((q_hbm, k_hbm, v_hbm))
    ]
    for load in loads:
        load.start()

    near = jnp.int32(0)
    ends = []
    for h in range(heads):
        kind = kind_ref[h]
        inverse[h] = jnp.where(kind == 0, near, HS + h - near)
        near = near + (1 - kind)
        ends.append(near)

    def find(r, carry):
        first = jnp.int32(0)
        second = jnp.int32(0)
        for h in range(heads):
            first = first + jnp.where(ends[h] <= r, 1, 0)
            second = second + jnp.where(h + 1 - ends[h] <= r - HS, 1, 0)
        order[r] = jnp.minimum(jnp.where(r < HS, first, second), heads - 1)
        return carry

    lax.fori_loop(0, heads, find, 0)

    def space_copy(j, d):
        peer = flip(me, d, groups)
        return pltpu.make_async_remote_copy(
            src_ref=packed.at[peer * owned + j],
            dst_ref=seen.at[j, me],
            send_sem=space_send.at[j, d],
            recv_sem=space_recv.at[j, d],
            device_id={"grp": peer},
            device_id_type=MESH,
        )

    def back_copy(j, d):
        peer = flip(me, d, groups)
        return pltpu.make_async_remote_copy(
            src_ref=made.at[j, peer],
            dst_ref=result.at[me * owned + j],
            send_sem=back_send.at[j, d],
            recv_sem=back_recv.at[j, d],
            device_id={"grp": peer},
            device_id_type=MESH,
        )

    def rows_of(unit):
        if splits == 1:
            return pl.ds(0, rows)
        return pl.ds(pl.multiple_of(lax.rem(unit, jnp.int32(splits)) * rows, rows), rows)

    def time_copy(d):
        peer = flip(frame, d, frames)
        return pltpu.make_async_remote_copy(
            src_ref=packed_time.at[peer],
            dst_ref=seen_time.at[frame],
            send_sem=time_send.at[d],
            recv_sem=time_recv.at[d],
            device_id={"blk": peer},
            device_id_type=MESH,
        )

    def home_copy(d):
        peer = flip(frame, d, frames)
        return pltpu.make_async_remote_copy(
            src_ref=made_time.at[peer],
            dst_ref=result.at[HS + lax.div(frame, jnp.int32(splits)), rows_of(frame)],
            send_sem=home_send.at[d],
            recv_sem=home_recv.at[d],
            device_id={"blk": peer},
            device_id_type=MESH,
        )

    pl.semaphore_wait(barrier, len(space_peers) + len(time_peers))
    for load in loads:
        load.wait()

    def send_space(j):
        for d in space_peers:
            rank = flip(me, d, groups) * owned + j
            for part in range(3):
                packed[rank, part] = stage[part, order[rank]]
            space_copy(j, d).start()

    def pack_time(unit, target, slot):
        head = order[HS + lax.div(unit, jnp.int32(splits))]
        for part in range(3):
            target[slot, part] = stage[part, head, rows_of(unit)]

    send_space(0)
    for d in time_peers:
        peer = flip(frame, d, frames)
        pack_time(peer, packed_time, peer)
        time_copy(d).start()
    for j in range(1, owned):
        send_space(j)
    for j in range(owned):
        for part in range(3):
            seen[j, me, part] = stage[part, order[me * owned + j]]
    pack_time(frame, seen_time, frame)

    def space_head(j):
        for d in space_peers:
            space_copy(j, d).wait_recv()

        def block(step, carry):
            d = lax.rem(step + groups // 2, jnp.int32(groups))
            peer = flip(me, d, groups)
            made[j, peer] = weighted(
                seen[j, peer, 0],
                seen[j, :, 1].reshape(groups * places, size),
                seen[j, :, 2].reshape(groups * places, size),
                factor,
            )

            @pl.when(d != 0)
            def _():
                back_copy(j, d).start()

            return carry

        lax.fori_loop(0, groups, block, 0)
        result[me * owned + j] = made[j, me]

    def time_head():
        for d in time_peers:
            time_copy(d).wait_recv()
        reach = reach_ref[order[HS + lax.div(frame, jnp.int32(splits))]]
        wide = 256 // frames
        tokens = frames * wide
        left = lax.broadcasted_iota(jnp.int32, (tokens, tokens), 0)
        right = lax.broadcasted_iota(jnp.int32, (tokens, tokens), 1)
        log = wide.bit_length() - 1
        distance = jnp.abs((left >> log) - (right >> log))
        allowed = ((left & (wide - 1)) == (right & (wide - 1))) & (distance <= reach)

        def piece(at, carry):
            part_rows = pl.ds(pl.multiple_of(at * wide, wide), wide)
            q, k, v = (
                seen_time[:, part, part_rows].reshape(tokens, size) for part in range(3)
            )
            made_time[:, part_rows] = weighted(q, k, v, factor, allowed).reshape(
                frames, wide, size
            )
            return carry

        lax.fori_loop(0, rows // wide, piece, 0)
        for d in time_peers:
            home_copy(d).start()
        result[HS + lax.div(frame, jnp.int32(splits)), rows_of(frame)] = made_time[frame]

    def heads_loop(j, carry):
        space_head(j)
        return carry

    lax.fori_loop(0, 1, heads_loop, 0)
    time_head()
    lax.fori_loop(1, owned, heads_loop, 0)

    for d in time_peers:
        time_copy(d).wait_send()
        home_copy(d).wait()
    for j in range(owned):
        for d in space_peers:
            space_copy(j, d).wait_send()
            back_copy(j, d).wait()
    for h in range(heads):
        out_ref[:, h * size : (h + 1) * size] = result[inverse[h]]


def body(groups, frames, queries, keys, values, head_kind, frame_reach):
    frames_here, places, width = queries.shape
    heads = head_kind.shape[0]
    size = width // heads
    owned = HS // groups
    splits = frames // (heads - HS)
    assert frames_here == 1 and owned * groups == HS and splits * (heads - HS) == frames
    rows = places // splits
    bf16 = jnp.bfloat16
    out = pl.pallas_call(
        functools.partial(kernel, groups, frames),
        out_shape=jax.ShapeDtypeStruct((places, width), bf16),
        in_specs=[pl.BlockSpec(memory_space=pl.ANY)] * 3
        + [pl.BlockSpec(memory_space=pltpu.SMEM)] * 2,
        out_specs=pl.BlockSpec(memory_space=pltpu.VMEM),
        scratch_shapes=[
            pltpu.VMEM((3, heads, places, size), bf16),
            pltpu.VMEM((HS, 3, places, size), bf16),
            pltpu.VMEM((frames, 3, rows, size), bf16),
            pltpu.VMEM((owned, groups, 3, places, size), bf16),
            pltpu.VMEM((frames, 3, rows, size), bf16),
            pltpu.VMEM((owned, groups, places, size), bf16),
            pltpu.VMEM((frames, rows, size), bf16),
            pltpu.VMEM((heads, places, size), bf16),
            pltpu.SMEM((heads,), jnp.int32),
            pltpu.SMEM((heads,), jnp.int32),
            pltpu.SemaphoreType.DMA((3, heads)),
            pltpu.SemaphoreType.DMA((owned, groups)),
            pltpu.SemaphoreType.DMA((owned, groups)),
            pltpu.SemaphoreType.DMA((owned, groups)),
            pltpu.SemaphoreType.DMA((owned, groups)),
            pltpu.SemaphoreType.DMA((frames,)),
            pltpu.SemaphoreType.DMA((frames,)),
            pltpu.SemaphoreType.DMA((frames,)),
            pltpu.SemaphoreType.DMA((frames,)),
        ],
        compiler_params=pltpu.CompilerParams(
            collective_id=0, has_side_effects=True, vmem_limit_bytes=48 * 1024 * 1024
        ),
        name="exchange_attend",
    )(queries[0], keys[0], values[0], head_kind, frame_reach)
    return out[None]


def solution(mesh):
    placed = (P("blk", "grp", None), P("blk", "grp", None), P("blk", "grp", None), P(), P())
    return jax.shard_map(
        functools.partial(body, mesh.shape["grp"], mesh.shape["blk"]),
        mesh=mesh,
        in_specs=placed,
        out_specs=P("blk", "grp", None),
        check_vma=False,
    )
```

```python
import functools

import jax
import jax.numpy as jnp
from jax import lax
from jax.experimental import pallas as pl
from jax.experimental.pallas import tpu as pltpu
from jax.sharding import PartitionSpec as P

HS = 16
MESH = pl.DeviceIdType.MESH


def flip(me, other, size):
    total, place = 0, 1
    while place < size:
        mine = lax.rem(lax.div(me, jnp.int32(place)), jnp.int32(2))
        if isinstance(other, int):
            digit = (other // place) % 2
            changed = 1 - mine if digit else mine
        else:
            digit = lax.rem(lax.div(other, jnp.int32(place)), jnp.int32(2))
            changed = lax.rem(mine + digit, jnp.int32(2))
        total = total + place * changed
        place *= 2
    return total


def far_first(size):
    return [(step + size // 2) % size for step in range(size) if (step + size // 2) % size]


def weighted(q, k, v, factor, allowed=None):
    scores = lax.dot_general(q, k, (((1,), (1,)), ((), ())), preferred_element_type=jnp.float32)
    if allowed is not None:
        scores = jnp.where(allowed, scores, -1e30)
    top = jnp.max(scores, axis=-1, keepdims=True)
    weights = jnp.exp((scores - top) * factor)
    total = jnp.sum(weights, axis=-1, keepdims=True)
    summed = jnp.dot(weights.astype(jnp.bfloat16), v, preferred_element_type=jnp.float32)
    return (summed / total).astype(jnp.bfloat16)


def kernel(
    groups, frames,
    q_hbm, k_hbm, v_hbm, kind_hbm, reach_hbm, out_ref,
    stage, packed, packed_time, seen, seen_time, made, made_time, result,
    kind_ref, reach_ref, order, inverse, following,
    small_sem, load_sem, space_send, space_recv, back_send, back_recv,
    time_send, time_recv, home_send, home_recv,
):
    heads = kind_ref.shape[0]
    places = stage.shape[2]
    size = stage.shape[3]
    owned = HS // groups
    splits = frames // (heads - HS)
    rows = places // splits
    factor = size ** (-0.5)
    me = lax.axis_index("grp")
    frame = lax.axis_index("blk")
    space_peers = far_first(groups)
    time_peers = far_first(frames)

    barrier = pltpu.get_barrier_semaphore()
    for d in space_peers:
        pl.semaphore_signal(
            barrier, inc=1, device_id={"grp": flip(me, d, groups)}, device_id_type=MESH
        )
    for d in time_peers:
        pl.semaphore_signal(
            barrier, inc=1, device_id={"blk": flip(frame, d, frames)}, device_id_type=MESH
        )
    smalls = [
        pltpu.make_async_copy(kind_hbm, kind_ref, small_sem.at[0]),
        pltpu.make_async_copy(reach_hbm, reach_ref, small_sem.at[1]),
    ]
    for small in smalls:
        small.start()
    loads = [
        pltpu.make_async_copy(
            source.at[:, h * size : (h + 1) * size], stage.at[part, h], load_sem.at[part, h]
        )
        for h in range(heads)
        for part, source in enumerate((q_hbm, k_hbm, v_hbm))
    ]
    for load in loads:
        load.start()

    for small in smalls:
        small.wait()

    near = jnp.int32(0)
    for h in range(heads):
        kind = kind_ref[h]
        inverse[h] = jnp.where(kind == 0, near, HS + h - near)
        near = near + (1 - kind)
    upcoming = [jnp.int32(heads - 1)] * 2
    for h in range(heads, -1, -1):
        if h < heads:
            kind = kind_ref[h]
            upcoming = [jnp.where(kind == want, h, upcoming[want]) for want in range(2)]
        for want in range(2):
            following[want, h] = upcoming[want]
    for want, first, last in ((0, 0, HS), (1, HS, heads)):
        head = following[want, 0]
        for r in range(first, last):
            order[r] = head
            if r + 1 < last:
                head = following[want, head + 1]

    def space_copy(j, d):
        peer = flip(me, d, groups)
        return pltpu.make_async_remote_copy(
            src_ref=packed.at[peer * owned + j],
            dst_ref=seen.at[j, me],
            send_sem=space_send.at[j, d],
            recv_sem=space_recv.at[j, d],
            device_id={"grp": peer},
            device_id_type=MESH,
        )

    def back_copy(j, d):
        peer = flip(me, d, groups)
        return pltpu.make_async_remote_copy(
            src_ref=made.at[j, peer],
            dst_ref=result.at[me * owned + j],
            send_sem=back_send.at[j, d],
            recv_sem=back_recv.at[j, d],
            device_id={"grp": peer},
            device_id_type=MESH,
        )

    def rows_of(unit):
        if splits == 1:
            return pl.ds(0, rows)
        return pl.ds(pl.multiple_of(lax.rem(unit, jnp.int32(splits)) * rows, rows), rows)

    def time_copy(d):
        peer = flip(frame, d, frames)
        return pltpu.make_async_remote_copy(
            src_ref=packed_time.at[peer],
            dst_ref=seen_time.at[frame],
            send_sem=time_send.at[d],
            recv_sem=time_recv.at[d],
            device_id={"blk": peer},
            device_id_type=MESH,
        )

    def home_copy(d):
        peer = flip(frame, d, frames)
        return pltpu.make_async_remote_copy(
            src_ref=made_time.at[peer],
            dst_ref=result.at[HS + lax.div(frame, jnp.int32(splits)), rows_of(frame)],
            send_sem=home_send.at[d],
            recv_sem=home_recv.at[d],
            device_id={"blk": peer},
            device_id_type=MESH,
        )

    pl.semaphore_wait(barrier, len(space_peers) + len(time_peers))
    for load in loads:
        load.wait()

    def send_space(j):
        for d in space_peers:
            rank = flip(me, d, groups) * owned + j
            for part in range(3):
                packed[rank, part] = stage[part, order[rank]]
            space_copy(j, d).start()

    def pack_time(unit, target, slot):
        head = order[HS + lax.div(unit, jnp.int32(splits))]
        for part in range(3):
            target[slot, part] = stage[part, head, rows_of(unit)]

    send_space(0)
    for d in time_peers:
        peer = flip(frame, d, frames)
        pack_time(peer, packed_time, peer)
        time_copy(d).start()
    for j in range(1, owned):
        send_space(j)
    for j in range(owned):
        for part in range(3):
            seen[j, me, part] = stage[part, order[me * owned + j]]
    pack_time(frame, seen_time, frame)

    def space_head(j):
        for d in space_peers:
            space_copy(j, d).wait_recv()

        def block(step, carry):
            d = lax.rem(step + groups // 2, jnp.int32(groups))
            peer = flip(me, d, groups)
            made[j, peer] = weighted(
                seen[j, peer, 0],
                seen[j, :, 1].reshape(groups * places, size),
                seen[j, :, 2].reshape(groups * places, size),
                factor,
            )

            @pl.when(d != 0)
            def _():
                back_copy(j, d).start()

            return carry

        lax.fori_loop(0, groups, block, 0)
        result[me * owned + j] = made[j, me]

    def time_head():
        for d in time_peers:
            time_copy(d).wait_recv()
        reach = reach_ref[order[HS + lax.div(frame, jnp.int32(splits))]]
        wide = 256 // frames
        tokens = frames * wide
        left = lax.broadcasted_iota(jnp.int32, (tokens, tokens), 0)
        right = lax.broadcasted_iota(jnp.int32, (tokens, tokens), 1)
        log = wide.bit_length() - 1
        distance = jnp.abs((left >> log) - (right >> log))
        allowed = ((left & (wide - 1)) == (right & (wide - 1))) & (distance <= reach)

        def piece(at, carry):
            part_rows = pl.ds(pl.multiple_of(at * wide, wide), wide)
            q, k, v = (
                seen_time[:, part, part_rows].reshape(tokens, size) for part in range(3)
            )
            made_time[:, part_rows] = weighted(q, k, v, factor, allowed).reshape(
                frames, wide, size
            )
            return carry

        lax.fori_loop(0, rows // wide, piece, 0)
        for d in time_peers:
            home_copy(d).start()
        result[HS + lax.div(frame, jnp.int32(splits)), rows_of(frame)] = made_time[frame]

    def heads_loop(j, carry):
        space_head(j)
        return carry

    lax.fori_loop(0, 1, heads_loop, 0)
    time_head()
    lax.fori_loop(1, owned, heads_loop, 0)

    for d in time_peers:
        time_copy(d).wait_send()
        home_copy(d).wait()
    for j in range(owned):
        for d in space_peers:
            space_copy(j, d).wait_send()
            back_copy(j, d).wait()
    for h in range(heads):
        out_ref[:, h * size : (h + 1) * size] = result[inverse[h]]


def body(groups, frames, queries, keys, values, head_kind, frame_reach):
    frames_here, places, width = queries.shape
    heads = head_kind.shape[0]
    size = width // heads
    owned = HS // groups
    splits = frames // (heads - HS)
    assert frames_here == 1 and owned * groups == HS and splits * (heads - HS) == frames
    rows = places // splits
    bf16 = jnp.bfloat16
    out = pl.pallas_call(
        functools.partial(kernel, groups, frames),
        out_shape=jax.ShapeDtypeStruct((places, width), bf16),
        in_specs=[pl.BlockSpec(memory_space=pltpu.HBM)] * 5,
        out_specs=pl.BlockSpec(memory_space=pltpu.VMEM),
        scratch_shapes=[
            pltpu.VMEM((3, heads, places, size), bf16),
            pltpu.VMEM((HS, 3, places, size), bf16),
            pltpu.VMEM((frames, 3, rows, size), bf16),
            pltpu.VMEM((owned, groups, 3, places, size), bf16),
            pltpu.VMEM((frames, 3, rows, size), bf16),
            pltpu.VMEM((owned, groups, places, size), bf16),
            pltpu.VMEM((frames, rows, size), bf16),
            pltpu.VMEM((heads, places, size), bf16),
            pltpu.SMEM((heads,), jnp.int32),
            pltpu.SMEM((heads,), jnp.int32),
            pltpu.SMEM((heads,), jnp.int32),
            pltpu.SMEM((heads,), jnp.int32),
            pltpu.SMEM((2, heads + 1), jnp.int32),
            pltpu.SemaphoreType.DMA((2,)),
            pltpu.SemaphoreType.DMA((3, heads)),
            pltpu.SemaphoreType.DMA((owned, groups)),
            pltpu.SemaphoreType.DMA((owned, groups)),
            pltpu.SemaphoreType.DMA((owned, groups)),
            pltpu.SemaphoreType.DMA((owned, groups)),
            pltpu.SemaphoreType.DMA((frames,)),
            pltpu.SemaphoreType.DMA((frames,)),
            pltpu.SemaphoreType.DMA((frames,)),
            pltpu.SemaphoreType.DMA((frames,)),
        ],
        compiler_params=pltpu.CompilerParams(
            collective_id=0, has_side_effects=True, vmem_limit_bytes=60 * 1024 * 1024
        ),
        name="exchange_attend",
    )(queries[0], keys[0], values[0], head_kind, frame_reach)
    return out[None]


def solution(mesh):
    placed = (P("blk", "grp", None), P("blk", "grp", None), P("blk", "grp", None), P(), P())
    return jax.shard_map(
        functools.partial(body, mesh.shape["grp"], mesh.shape["blk"]),
        mesh=mesh,
        in_specs=placed,
        out_specs=P("blk", "grp", None),
        check_vma=False,
    )
```

```python
import functools

import jax
import jax.numpy as jnp
from jax import lax
from jax.experimental import pallas as pl
from jax.experimental.pallas import tpu as pltpu
from jax.sharding import PartitionSpec as P

HS = 16
MESH = pl.DeviceIdType.MESH


def flip(me, other, size):
    total, place = 0, 1
    while place < size:
        mine = lax.rem(lax.div(me, jnp.int32(place)), jnp.int32(2))
        if isinstance(other, int):
            digit = (other // place) % 2
            changed = 1 - mine if digit else mine
        else:
            digit = lax.rem(lax.div(other, jnp.int32(place)), jnp.int32(2))
            changed = lax.rem(mine + digit, jnp.int32(2))
        total = total + place * changed
        place *= 2
    return total


def far_first(size):
    return [(step + size // 2) % size for step in range(size) if (step + size // 2) % size]


def weighted(q, k, v, factor, allowed=None):
    scores = lax.dot_general(q, k, (((1,), (1,)), ((), ())), preferred_element_type=jnp.float32)
    if allowed is not None:
        scores = jnp.where(allowed, scores, -1e30)
    top = jnp.max(scores, axis=-1, keepdims=True)
    weights = jnp.exp((scores - top) * factor)
    total = jnp.sum(weights, axis=-1, keepdims=True)
    summed = jnp.dot(weights.astype(jnp.bfloat16), v, preferred_element_type=jnp.float32)
    return (summed / total).astype(jnp.bfloat16)


def kernel(
    groups, frames,
    q_hbm, k_hbm, v_hbm, kind_hbm, reach_hbm, out_ref,
    stage, packed, packed_time, seen, seen_time, made, made_time, result,
    kind_ref, reach_ref, order, inverse, following,
    small_sem, load_sem, space_send, space_recv, back_send, back_recv,
    time_send, time_recv, home_send, home_recv,
):
    heads = kind_ref.shape[0]
    places = stage.shape[2]
    size = stage.shape[3]
    owned = HS // groups
    splits = frames // (heads - HS)
    rows = places // splits
    factor = size ** (-0.5)
    me = lax.axis_index("grp")
    frame = lax.axis_index("blk")
    space_peers = far_first(groups)
    time_peers = far_first(frames)

    barrier = pltpu.get_barrier_semaphore()
    for d in space_peers:
        pl.semaphore_signal(
            barrier, inc=1, device_id={"grp": flip(me, d, groups)}, device_id_type=MESH
        )
    for d in time_peers:
        pl.semaphore_signal(
            barrier, inc=1, device_id={"blk": flip(frame, d, frames)}, device_id_type=MESH
        )
    smalls = [
        pltpu.make_async_copy(kind_hbm, kind_ref, small_sem.at[0]),
        pltpu.make_async_copy(reach_hbm, reach_ref, small_sem.at[1]),
    ]
    for small in smalls:
        small.start()
    loads = [
        pltpu.make_async_copy(
            source.at[:, h * size : (h + 1) * size], stage.at[part, h], load_sem.at[part, h]
        )
        for h in range(heads)
        for part, source in enumerate((q_hbm, k_hbm, v_hbm))
    ]
    for load in loads:
        load.start()

    for small in smalls:
        small.wait()

    near = jnp.int32(0)
    for h in range(heads):
        kind = kind_ref[h]
        inverse[h] = jnp.where(kind == 0, near, HS + h - near)
        near = near + (1 - kind)
    upcoming = [jnp.int32(heads - 1)] * 2
    for h in range(heads, -1, -1):
        if h < heads:
            kind = kind_ref[h]
            upcoming = [jnp.where(kind == want, h, upcoming[want]) for want in range(2)]
        for want in range(2):
            following[want, h] = upcoming[want]
    for want, first, last in ((0, 0, HS), (1, HS, heads)):
        head = following[want, 0]
        for r in range(first, last):
            order[r] = head
            if r + 1 < last:
                head = following[want, head + 1]

    def space_copy(j, d):
        peer = flip(me, d, groups)
        return pltpu.make_async_remote_copy(
            src_ref=packed.at[peer * owned + j],
            dst_ref=seen.at[j, me],
            send_sem=space_send.at[j, d],
            recv_sem=space_recv.at[j, d],
            device_id={"grp": peer},
            device_id_type=MESH,
        )

    def back_copy(j, d):
        peer = flip(me, d, groups)
        return pltpu.make_async_remote_copy(
            src_ref=made.at[j, peer],
            dst_ref=result.at[me * owned + j],
            send_sem=back_send.at[j, d],
            recv_sem=back_recv.at[j, d],
            device_id={"grp": peer},
            device_id_type=MESH,
        )

    def rows_of(unit):
        if splits == 1:
            return pl.ds(0, rows)
        return pl.ds(pl.multiple_of(lax.rem(unit, jnp.int32(splits)) * rows, rows), rows)

    def time_copy(d):
        peer = flip(frame, d, frames)
        return pltpu.make_async_remote_copy(
            src_ref=packed_time.at[peer],
            dst_ref=seen_time.at[frame],
            send_sem=time_send.at[d],
            recv_sem=time_recv.at[d],
            device_id={"blk": peer},
            device_id_type=MESH,
        )

    def home_copy(d):
        peer = flip(frame, d, frames)
        return pltpu.make_async_remote_copy(
            src_ref=made_time.at[peer],
            dst_ref=result.at[HS + lax.div(frame, jnp.int32(splits)), rows_of(frame)],
            send_sem=home_send.at[d],
            recv_sem=home_recv.at[d],
            device_id={"blk": peer},
            device_id_type=MESH,
        )

    pl.semaphore_wait(barrier, len(space_peers) + len(time_peers))
    for load in loads:
        load.wait()

    def send_space(j):
        for d in space_peers:
            rank = flip(me, d, groups) * owned + j
            for part in range(3):
                packed[rank, part] = stage[part, order[rank]]
            space_copy(j, d).start()

    def pack_time(unit, target, slot):
        head = order[HS + lax.div(unit, jnp.int32(splits))]
        for part in range(3):
            target[slot, part] = stage[part, head, rows_of(unit)]

    send_space(0)
    for d in time_peers:
        peer = flip(frame, d, frames)
        pack_time(peer, packed_time, peer)
        time_copy(d).start()
    for j in range(1, owned):
        send_space(j)
    for j in range(owned):
        for part in range(3):
            seen[j, me, part] = stage[part, order[me * owned + j]]
    pack_time(frame, seen_time, frame)

    def space_head(j):
        for d in space_peers:
            space_copy(j, d).wait_recv()

        def block(step, carry):
            d = lax.rem(step + groups // 2, jnp.int32(groups))
            peer = flip(me, d, groups)
            made[j, peer] = weighted(
                seen[j, peer, 0],
                seen[j, :, 1].reshape(groups * places, size),
                seen[j, :, 2].reshape(groups * places, size),
                factor,
            )

            @pl.when(d != 0)
            def _():
                back_copy(j, d).start()

            return carry

        lax.fori_loop(0, groups, block, 0)
        result[me * owned + j] = made[j, me]

    def time_head():
        for d in time_peers:
            time_copy(d).wait_recv()
        reach = reach_ref[order[HS + lax.div(frame, jnp.int32(splits))]]
        wide = 256 // frames
        tokens = frames * wide
        left = lax.broadcasted_iota(jnp.int32, (tokens, tokens), 0)
        right = lax.broadcasted_iota(jnp.int32, (tokens, tokens), 1)
        log = wide.bit_length() - 1
        distance = jnp.abs((left >> log) - (right >> log))
        allowed = ((left & (wide - 1)) == (right & (wide - 1))) & (distance <= reach)

        def piece(at, carry):
            part_rows = pl.ds(pl.multiple_of(at * wide, wide), wide)
            q, k, v = (
                seen_time[:, part, part_rows].reshape(tokens, size) for part in range(3)
            )
            made_time[:, part_rows] = weighted(q, k, v, factor, allowed).reshape(
                frames, wide, size
            )
            return carry

        lax.fori_loop(0, rows // wide, piece, 0)
        for d in time_peers:
            home_copy(d).start()
        result[HS + lax.div(frame, jnp.int32(splits)), rows_of(frame)] = made_time[frame]

    def heads_loop(j, carry):
        space_head(j)
        return carry

    lax.fori_loop(0, 1, heads_loop, 0)
    time_head()
    lax.fori_loop(1, owned, heads_loop, 0)

    for d in time_peers:
        time_copy(d).wait_send()
        home_copy(d).wait()
    for j in range(owned):
        for d in space_peers:
            space_copy(j, d).wait_send()
            back_copy(j, d).wait()
    for h in range(heads):
        out_ref[:, h * size : (h + 1) * size] = result[inverse[h]]


def body(groups, frames, queries, keys, values, head_kind, frame_reach):
    frames_here, places, width = queries.shape
    heads = head_kind.shape[0]
    size = width // heads
    owned = HS // groups
    splits = frames // (heads - HS)
    assert frames_here == 1 and owned * groups == HS and splits * (heads - HS) == frames
    rows = places // splits
    bf16 = jnp.bfloat16
    out = pl.pallas_call(
        functools.partial(kernel, groups, frames),
        out_shape=jax.ShapeDtypeStruct((places, width), bf16),
        in_specs=[pl.BlockSpec(memory_space=pltpu.HBM)] * 5,
        out_specs=pl.BlockSpec(memory_space=pltpu.VMEM),
        scratch_shapes=[
            pltpu.VMEM((3, heads, places, size), bf16),
            pltpu.VMEM((HS, 3, places, size), bf16),
            pltpu.VMEM((frames, 3, rows, size), bf16),
            pltpu.VMEM((owned, groups, 3, places, size), bf16),
            pltpu.VMEM((frames, 3, rows, size), bf16),
            pltpu.VMEM((owned, groups, places, size), bf16),
            pltpu.VMEM((frames, rows, size), bf16),
            pltpu.VMEM((heads, places, size), bf16),
            pltpu.SMEM((heads,), jnp.int32),
            pltpu.SMEM((heads,), jnp.int32),
            pltpu.SMEM((heads,), jnp.int32),
            pltpu.SMEM((heads,), jnp.int32),
            pltpu.SMEM((2, heads + 1), jnp.int32),
            pltpu.SemaphoreType.DMA((2,)),
            pltpu.SemaphoreType.DMA((3, heads)),
            pltpu.SemaphoreType.DMA((owned, groups)),
            pltpu.SemaphoreType.DMA((owned, groups)),
            pltpu.SemaphoreType.DMA((owned, groups)),
            pltpu.SemaphoreType.DMA((owned, groups)),
            pltpu.SemaphoreType.DMA((frames,)),
            pltpu.SemaphoreType.DMA((frames,)),
            pltpu.SemaphoreType.DMA((frames,)),
            pltpu.SemaphoreType.DMA((frames,)),
        ],
        compiler_params=pltpu.CompilerParams(
            collective_id=0, has_side_effects=True, vmem_limit_bytes=48 * 1024 * 1024
        ),
        name="exchange_attend",
    )(
        *(
            pltpu.with_memory_space_constraint(operand, pltpu.HBM)
            for operand in (queries[0], keys[0], values[0], head_kind, frame_reach)
        )
    )
    return out[None]


def solution(mesh):
    placed = (P("blk", "grp", None), P("blk", "grp", None), P("blk", "grp", None), P(), P())
    return jax.shard_map(
        functools.partial(body, mesh.shape["grp"], mesh.shape["blk"]),
        mesh=mesh,
        in_specs=placed,
        out_specs=P("blk", "grp", None),
        check_vma=False,
    )
```

```python
import functools

import jax
import jax.numpy as jnp
from jax import lax
from jax.experimental import pallas as pl
from jax.experimental.pallas import tpu as pltpu
from jax.sharding import PartitionSpec as P

HS = 16
MESH = pl.DeviceIdType.MESH


def flip(me, other, size):
    total, place = 0, 1
    while place < size:
        mine = lax.rem(lax.div(me, jnp.int32(place)), jnp.int32(2))
        if isinstance(other, int):
            digit = (other // place) % 2
            changed = 1 - mine if digit else mine
        else:
            digit = lax.rem(lax.div(other, jnp.int32(place)), jnp.int32(2))
            changed = lax.rem(mine + digit, jnp.int32(2))
        total = total + place * changed
        place *= 2
    return total


def far_first(size):
    return [(step + size // 2) % size for step in range(size) if (step + size // 2) % size]


def weighted(q, k, v, factor, allowed=None):
    scores = lax.dot_general(q, k, (((1,), (1,)), ((), ())), preferred_element_type=jnp.float32)
    if allowed is not None:
        scores = jnp.where(allowed, scores, -1e30)
    top = jnp.max(scores, axis=-1, keepdims=True)
    weights = jnp.exp((scores - top) * factor)
    total = jnp.sum(weights, axis=-1, keepdims=True)
    summed = jnp.dot(weights.astype(jnp.bfloat16), v, preferred_element_type=jnp.float32)
    return (summed / total).astype(jnp.bfloat16)


def kernel(
    groups, frames,
    q_hbm, k_hbm, v_hbm, kind_hbm, reach_hbm, out_ref,
    stage_q, stage_k, stage_v, packed, packed_time, seen, seen_time, made, made_time, result,
    kind_ref, reach_ref, order, inverse, following,
    small_sem, load_sem, first_send, first_recv, space_send, space_recv, back_send, back_recv,
    time_send, time_recv, home_send, home_recv,
):
    heads = kind_ref.shape[0]
    stage = (stage_q, stage_k, stage_v)
    places = stage_q.shape[1]
    size = stage_q.shape[2]
    owned = HS // groups
    splits = frames // (heads - HS)
    rows = places // splits
    factor = size ** (-0.5)
    me = lax.axis_index("grp")
    frame = lax.axis_index("blk")
    space_peers = far_first(groups)
    time_peers = far_first(frames)

    barrier = pltpu.get_barrier_semaphore()
    for d in space_peers:
        pl.semaphore_signal(
            barrier, inc=1, device_id={"grp": flip(me, d, groups)}, device_id_type=MESH
        )
    for d in time_peers:
        pl.semaphore_signal(
            barrier, inc=1, device_id={"blk": flip(frame, d, frames)}, device_id_type=MESH
        )
    smalls = [
        pltpu.make_async_copy(kind_hbm, kind_ref, small_sem.at[0]),
        pltpu.make_async_copy(reach_hbm, reach_ref, small_sem.at[1]),
    ]
    for small in smalls:
        small.start()
    loads = [
        pltpu.make_async_copy(
            source.at[:, h * size : (h + 1) * size], stage[part].at[h], load_sem.at[part, h]
        )
        for part, source in enumerate((q_hbm, k_hbm, v_hbm))
        for h in range(heads)
    ]
    for load in loads:
        load.start()

    for small in smalls:
        small.wait()

    near = jnp.int32(0)
    for h in range(heads):
        kind = kind_ref[h]
        inverse[h] = jnp.where(kind == 0, near, HS + h - near)
        near = near + (1 - kind)
    upcoming = [jnp.int32(heads - 1)] * 2
    for h in range(heads, -1, -1):
        if h < heads:
            kind = kind_ref[h]
            upcoming = [jnp.where(kind == want, h, upcoming[want]) for want in range(2)]
        for want in range(2):
            following[want, h] = upcoming[want]
    for want, first, last in ((0, 0, HS), (1, HS, heads)):
        head = following[want, 0]
        for r in range(first, last):
            order[r] = head
            if r + 1 < last:
                head = following[want, head + 1]

    def space_copy(j, d):
        peer = flip(me, d, groups)
        return pltpu.make_async_remote_copy(
            src_ref=packed.at[peer * owned + j],
            dst_ref=seen.at[j, me],
            send_sem=space_send.at[j, d],
            recv_sem=space_recv.at[j, d],
            device_id={"grp": peer},
            device_id_type=MESH,
        )

    def first_copy(part, d):
        peer = flip(me, d, groups)
        return pltpu.make_async_remote_copy(
            src_ref=packed.at[peer * owned, part],
            dst_ref=seen.at[0, me, part],
            send_sem=first_send.at[part, d],
            recv_sem=first_recv.at[part, d],
            device_id={"grp": peer},
            device_id_type=MESH,
        )

    def back_copy(j, d):
        peer = flip(me, d, groups)
        return pltpu.make_async_remote_copy(
            src_ref=made.at[j, peer],
            dst_ref=result.at[me * owned + j],
            send_sem=back_send.at[j, d],
            recv_sem=back_recv.at[j, d],
            device_id={"grp": peer},
            device_id_type=MESH,
        )

    def rows_of(unit):
        if splits == 1:
            return pl.ds(0, rows)
        return pl.ds(pl.multiple_of(lax.rem(unit, jnp.int32(splits)) * rows, rows), rows)

    def time_copy(d):
        peer = flip(frame, d, frames)
        return pltpu.make_async_remote_copy(
            src_ref=packed_time.at[peer],
            dst_ref=seen_time.at[frame],
            send_sem=time_send.at[d],
            recv_sem=time_recv.at[d],
            device_id={"blk": peer},
            device_id_type=MESH,
        )

    def home_copy(d):
        peer = flip(frame, d, frames)
        return pltpu.make_async_remote_copy(
            src_ref=made_time.at[peer],
            dst_ref=result.at[HS + lax.div(frame, jnp.int32(splits)), rows_of(frame)],
            send_sem=home_send.at[d],
            recv_sem=home_recv.at[d],
            device_id={"blk": peer},
            device_id_type=MESH,
        )

    pl.semaphore_wait(barrier, len(space_peers) + len(time_peers))

    def send_space(j):
        for d in space_peers:
            rank = flip(me, d, groups) * owned + j
            for part in range(3):
                packed[rank, part] = stage[part][order[rank]]
            space_copy(j, d).start()

    def pack_time(unit, target, slot):
        head = order[HS + lax.div(unit, jnp.int32(splits))]
        for part in range(3):
            target[slot, part] = stage[part][head, rows_of(unit)]

    for part in range(3):
        for load in loads[part * heads : (part + 1) * heads]:
            load.wait()
        for d in space_peers:
            rank = flip(me, d, groups) * owned
            packed[rank, part] = stage[part][order[rank]]
            first_copy(part, d).start()
    for d in time_peers:
        peer = flip(frame, d, frames)
        pack_time(peer, packed_time, peer)
        time_copy(d).start()
    for j in range(1, owned):
        send_space(j)
    for j in range(owned):
        for part in range(3):
            seen[j, me, part] = stage[part][order[me * owned + j]]
    pack_time(frame, seen_time, frame)

    def space_head(j):
        def block(step, carry):
            d = lax.rem(step + groups // 2, jnp.int32(groups))
            peer = flip(me, d, groups)
            made[j, peer] = weighted(
                seen[j, peer, 0],
                seen[j, :, 1].reshape(groups * places, size),
                seen[j, :, 2].reshape(groups * places, size),
                factor,
            )

            @pl.when(d != 0)
            def _():
                back_copy(j, d).start()

            return carry

        lax.fori_loop(0, groups, block, 0)
        result[me * owned + j] = made[j, me]

    def time_head():
        for d in time_peers:
            time_copy(d).wait_recv()
        reach = reach_ref[order[HS + lax.div(frame, jnp.int32(splits))]]
        wide = 256 // frames
        tokens = frames * wide
        left = lax.broadcasted_iota(jnp.int32, (tokens, tokens), 0)
        right = lax.broadcasted_iota(jnp.int32, (tokens, tokens), 1)
        log = wide.bit_length() - 1
        distance = jnp.abs((left >> log) - (right >> log))
        allowed = ((left & (wide - 1)) == (right & (wide - 1))) & (distance <= reach)

        def piece(at, carry):
            part_rows = pl.ds(pl.multiple_of(at * wide, wide), wide)
            q, k, v = (
                seen_time[:, part, part_rows].reshape(tokens, size) for part in range(3)
            )
            made_time[:, part_rows] = weighted(q, k, v, factor, allowed).reshape(
                frames, wide, size
            )
            return carry

        lax.fori_loop(0, rows // wide, piece, 0)
        for d in time_peers:
            home_copy(d).start()
        result[HS + lax.div(frame, jnp.int32(splits)), rows_of(frame)] = made_time[frame]

    def heads_loop(j, carry):
        for d in space_peers:
            space_copy(j, d).wait_recv()
        space_head(j)
        return carry

    for d in space_peers:
        for part in range(3):
            first_copy(part, d).wait_recv()
    space_head(0)
    time_head()
    lax.fori_loop(1, owned, heads_loop, 0)

    for d in time_peers:
        time_copy(d).wait_send()
        home_copy(d).wait()
    for d in space_peers:
        for part in range(3):
            first_copy(part, d).wait_send()
    for j in range(owned):
        for d in space_peers:
            if j > 0:
                space_copy(j, d).wait_send()
            back_copy(j, d).wait()
    for h in range(heads):
        out_ref[:, h * size : (h + 1) * size] = result[inverse[h]]


def body(groups, frames, queries, keys, values, head_kind, frame_reach):
    frames_here, places, width = queries.shape
    heads = head_kind.shape[0]
    size = width // heads
    owned = HS // groups
    splits = frames // (heads - HS)
    assert frames_here == 1 and owned * groups == HS and splits * (heads - HS) == frames
    rows = places // splits
    bf16 = jnp.bfloat16
    out = pl.pallas_call(
        functools.partial(kernel, groups, frames),
        out_shape=jax.ShapeDtypeStruct((places, width), bf16),
        in_specs=[pl.BlockSpec(memory_space=pltpu.HBM)] * 5,
        out_specs=pl.BlockSpec(memory_space=pltpu.VMEM),
        scratch_shapes=[
            pltpu.VMEM((heads, places, size), bf16),
            pltpu.VMEM((heads, places, size), bf16),
            pltpu.VMEM((heads, places, size), bf16),
            pltpu.VMEM((HS, 3, places, size), bf16),
            pltpu.VMEM((frames, 3, rows, size), bf16),
            pltpu.VMEM((owned, groups, 3, places, size), bf16),
            pltpu.VMEM((frames, 3, rows, size), bf16),
            pltpu.VMEM((owned, groups, places, size), bf16),
            pltpu.VMEM((frames, rows, size), bf16),
            pltpu.VMEM((heads, places, size), bf16),
            pltpu.SMEM((heads,), jnp.int32),
            pltpu.SMEM((heads,), jnp.int32),
            pltpu.SMEM((heads,), jnp.int32),
            pltpu.SMEM((heads,), jnp.int32),
            pltpu.SMEM((2, heads + 1), jnp.int32),
            pltpu.SemaphoreType.DMA((2,)),
            pltpu.SemaphoreType.DMA((3, heads)),
            pltpu.SemaphoreType.DMA((3, groups)),
            pltpu.SemaphoreType.DMA((3, groups)),
            pltpu.SemaphoreType.DMA((owned, groups)),
            pltpu.SemaphoreType.DMA((owned, groups)),
            pltpu.SemaphoreType.DMA((owned, groups)),
            pltpu.SemaphoreType.DMA((owned, groups)),
            pltpu.SemaphoreType.DMA((frames,)),
            pltpu.SemaphoreType.DMA((frames,)),
            pltpu.SemaphoreType.DMA((frames,)),
            pltpu.SemaphoreType.DMA((frames,)),
        ],
        compiler_params=pltpu.CompilerParams(
            collective_id=0, has_side_effects=True, vmem_limit_bytes=48 * 1024 * 1024
        ),
        name="exchange_attend",
    )(
        *(
            pltpu.with_memory_space_constraint(operand, pltpu.HBM)
            for operand in (queries[0], keys[0], values[0], head_kind, frame_reach)
        )
    )
    return out[None]


def solution(mesh):
    placed = (P("blk", "grp", None), P("blk", "grp", None), P("blk", "grp", None), P(), P())
    return jax.shard_map(
        functools.partial(body, mesh.shape["grp"], mesh.shape["blk"]),
        mesh=mesh,
        in_specs=placed,
        out_specs=P("blk", "grp", None),
        check_vma=False,
    )
```
